32 devices in a mesh: group: 2 (over x), adapter: 16 (over z, y, core).
Axes of the slice: x: 2, y: 2, z: 4, core: 2. Of those that a mesh axis runs over, the one named last changes fastest.
Arguments:
- hidden: bfloat16 [4096, 8192], P(('group', 'adapter')), parts along dimension 0, may hold values from -6 to 6
- base_qkv: bfloat16 [4096, 10240], P(('group', 'adapter')), parts along dimension 0, may hold values from -6 to 6
- adapter_id: int32 [4096, 1], P(('group', 'adapter')), parts along dimension 0, may hold values from 0 to 15; in each aligned block of 128 rows (0 to 127, 128 to 255, ...) at most 16 rows name the same one
- shrink: bfloat16 [16, 8192, 192], P('adapter'), may hold values from -0.0625 to 0.0625
- expand_q: bfloat16 [16, 64, 8192], P('adapter'), may hold values from -0.75 to 0.75
- expand_kv: bfloat16 [16, 2, 64, 1024], P('adapter'), may hold values from -0.75 to 0.75
Outputs:
- qkv: bfloat16 [4096, 10240], P(('group', 'adapter')), parts along dimension 0
The draws below stay inside these ranges and needn't reach their ends.
There are 2 independent parts, one for each index of `group`. The reference program is written for one: setup_inputs(seed, part) draws one part's arguments, and reference() takes and returns one part's arrays. A program takes and returns all parts, laid end to end along the dimension named above; an argument that names none is the same for every part. Nothing has to cross between parts.
Inputs may be any that keep to these rules, and one draw needn't show every extreme that they name: `adapter_id`: within the rows of one device (aligned blocks of 128 rows) no adapter is named by more than 16 rows, and in some block one adapter is named by exactly 16 rows.
All inputs are finite; a program needn't handle non-finite values.
Results may differ from the reference program's by a relative error of at most 0.0052.
Values may be sent and summed in bfloat16 or wider, within the bound.
A program may use at most 64 MiB of HBM per device.

```python
import math
import jax
import jax.numpy as jnp
import numpy as np
from jax import lax

D = 8192
KVW = 1024
R = 64
ROW_DEV = 128
ROWS = 2048
ADAPTERS = 16
CAP = 16
QKV = 10240


def level_of(key, dims, shards, smallest, largest):
    def one(axis_at, shards_of):
        draws = jax.random.uniform(jax.random.fold_in(jax.random.fold_in(key, 6), axis_at), (shards_of,), jnp.float32, smallest / len(shards), largest / len(shards))
        return jnp.repeat(jnp.exp(draws), dims[axis_at] // shards_of).reshape((-1,) + (1,) * (len(dims) - axis_at - 1))

    loudness = one(*shards[0])
    for cut in shards[1:]:
        loudness = loudness * one(*cut)
    return loudness


def shared_out(own_key, own, number, rows, number_of, top, most, slope):
    ranking = jax.random.permutation(own_key, number_of)
    heavy_load, usual = load_shares(number_of, rows * top, most, slope, True), load_shares(number_of, rows * top, most, slope, False)
    places = jnp.arange(number_of)

    def named(lengths, rotation):
        used = int((lengths > 0).sum())
        fixed = max(1, used // 4)
        shifted = fixed + (places - fixed + rotation * (used - fixed)) % max(1, number_of - fixed)
        return jnp.zeros((number_of,), jnp.int32).at[ranking[jnp.where(places < fixed, places, shifted)]].set(jnp.asarray(lengths, jnp.int32))

    lengths = jnp.where(number % 4 == 0, named(heavy_load, number // 4), named(usual, number - number // 4 - 1))
    mixed = jax.random.permutation(jax.random.fold_in(own, 3), number_of)
    donor, receiver = mixed[0:number_of // 2 * 2:2], mixed[1:number_of // 2 * 2:2]
    slack = jnp.minimum(lengths[donor] - 1, most - lengths[receiver]) // 2
    slack = jnp.where((donor == ranking[0]) | (receiver == ranking[0]) | (lengths[receiver] == 0), 0, jnp.maximum(slack, 0))
    shifted = jax.random.randint(jax.random.fold_in(own, 4), (number_of // 2,), 0, 1 << 20) % (slack + 1)
    lengths = lengths.at[donor].add(-shifted).at[receiver].add(shifted)
    items = jnp.searchsorted(jnp.cumsum(lengths), jnp.arange(rows * top), side="right").astype(jnp.int32)
    listing = items.reshape(top, rows).T
    listing = listing[jax.random.permutation(jax.random.fold_in(own, 1), rows)]
    rotation = jax.random.randint(jax.random.fold_in(own, 2), (rows, 1), 0, top)
    return jnp.take_along_axis(listing, (jnp.arange(top)[None, :] + rotation) % top, axis=1)


def load_shares(amount, total, most, lean, full):
    loads = [(1 << 20) // math.isqrt(rank ** lean) + 1 for rank in range(1, amount + 1)]
    largest = most if full else min(most, max(-(-total // amount), total * loads[0] // sum(loads)))
    least = 1 if total - largest >= amount - 1 else 0
    holding, surplus = [largest] + [least] * (amount - 1), total - largest - least * (amount - 1)
    while surplus > 0:
        movable = [i for i in range(1, amount) if holding[i] < largest] or [i for i in range(1, amount) if holding[i] < most]
        mass, budget = sum([loads[i] for i in movable]), surplus
        for i in movable:
            extra = min(most - holding[i], max(1, budget * loads[i] // mass), surplus)
            holding[i] = holding[i] + extra
            surplus = surplus - extra
    return np.array(holding)


def noise(stream_key, shape, spread, most, cuts=(), kind=jnp.bfloat16):
    values = spread * jax.random.normal(stream_key, shape, jnp.float32)
    if cuts:
        values = values * level_of(stream_key, shape, cuts, -0.22, 0.18)
    return jnp.clip(values, -most, most).astype(kind)


def setup_inputs(seed: int = 0, part: int = 0) -> dict:
    splits = jax.random.split(jax.random.key(seed), 7)
    part_splits = jax.random.split(jax.random.fold_in(splits[6], part), 7)
    hidden = noise(part_splits[0], (ROWS, D), 1.0, 6.0, ((0, 16),))
    base_qkv = noise(part_splits[1], (ROWS, QKV), 1.0, 6.0, ((0, 16),))
    adapter_id_keys = jax.random.split(jax.random.fold_in(part_splits[2], 1), ROWS // ROW_DEV)
    adapter_id_turns = jax.random.permutation(jax.random.fold_in(part_splits[2], 3), ROWS // ROW_DEV)
    adapter_id = jax.vmap(lambda own, number: shared_out(jax.random.fold_in(part_splits[2], 2), own, number, ROW_DEV, ADAPTERS, 1, CAP, 2))(adapter_id_keys, adapter_id_turns).reshape((ROWS, 1))
    shrink = noise(splits[3], (ADAPTERS, D, 3 * R), D ** -0.5, 0.0625, ((0, 16),))
    expand_q = noise(splits[4], (ADAPTERS, R, D), R ** -0.5, 0.75, ((0, 16),))
    expand_kv = noise(splits[5], (ADAPTERS, 2, R, KVW), R ** -0.5, 0.75, ((0, 16),))
    return {"hidden": hidden, "base_qkv": base_qkv, "adapter_id": adapter_id, "shrink": shrink, "expand_q": expand_q, "expand_kv": expand_kv}


def reference(hidden, base_qkv, adapter_id, shrink, expand_q, expand_kv):
    def one_row(packed):
        hidden_row, adapter_of = packed
        latent = jnp.dot(hidden_row[None, :], shrink[adapter_of], preferred_element_type=jnp.float32).astype(jnp.bfloat16)
        query_delta = jnp.dot(latent[:, 0:R], expand_q[adapter_of], preferred_element_type=jnp.float32)
        key_delta = jnp.dot(latent[:, R:2 * R], expand_kv[adapter_of, 0], preferred_element_type=jnp.float32)
        value_delta = jnp.dot(latent[:, 2 * R:3 * R], expand_kv[adapter_of, 1], preferred_element_type=jnp.float32)
        joined = jnp.concatenate([query_delta, key_delta, value_delta], axis=1)
        return joined[0].astype(jnp.bfloat16)

    deltas = lax.map(one_row, (hidden, adapter_id[:, 0].astype(jnp.int32)))
    return (base_qkv.astype(jnp.float32) + deltas.astype(jnp.float32)).astype(jnp.bfloat16)
```

```python
import jax
import jax.numpy as jnp
from jax import lax
from jax.experimental import pallas as pl
from jax.experimental.pallas import tpu as pltpu
from jax.sharding import PartitionSpec as P

R = 64


def project(latent, weight):
    return jnp.einsum("sacr,are->sace", latent, weight, preferred_element_type=jnp.float32).astype(
        jnp.bfloat16
    )


def per_device(hidden, base_qkv, adapter_id, shrink, expand_q, expand_kv):
    peer_count = lax.axis_size("adapter")
    row_count = hidden.shape[0]
    owned_count = shrink.shape[0]
    model_width = hidden.shape[1]
    slot_cap = max(2, (2 * row_count + peer_count * owned_count - 1) // (peer_count * owned_count))
    row_adapter = adapter_id[:, 0]
    matches = (row_adapter[:, None] == row_adapter[None, :]).astype(jnp.int32)
    earlier = lax.broadcasted_iota(jnp.int32, (row_count, row_count), 0) < lax.broadcasted_iota(
        jnp.int32, (row_count, row_count), 1
    )
    rank_in = jnp.sum(matches * earlier.astype(jnp.int32), axis=0)
    slot_of = row_adapter * slot_cap + rank_in
    slot_count = peer_count * owned_count * slot_cap
    placer = (
        lax.broadcasted_iota(jnp.int32, (slot_count, row_count), 0) == slot_of[None, :]
    ).astype(jnp.bfloat16)
    outgoing = jnp.dot(placer, hidden, preferred_element_type=jnp.float32).astype(jnp.bfloat16)
    outgoing = outgoing.reshape(peer_count, owned_count, slot_cap, model_width)
    latent = jnp.einsum(
        "sacd,adr->sacr",
        lax.all_to_all(outgoing, "adapter", split_axis=0, concat_axis=0, tiled=True),
        shrink,
        preferred_element_type=jnp.float32,
    ).astype(jnp.bfloat16)
    query_delta = project(latent[..., 0:R], expand_q)
    key_delta = project(latent[..., R : 2 * R], expand_kv[:, 0])
    value_delta = project(latent[..., 2 * R : 3 * R], expand_kv[:, 1])
    joined = jnp.concatenate([query_delta, key_delta, value_delta], axis=3)
    returned = lax.all_to_all(joined, "adapter", split_axis=0, concat_axis=0, tiled=True)
    flattened = returned.reshape(slot_count, returned.shape[3])
    deltas = jnp.take(flattened, slot_of, axis=0)
    return (base_qkv.astype(jnp.float32) + deltas.astype(jnp.float32)).astype(jnp.bfloat16)


Z, Y, C = 4, 2, 2
PEERS = Z * Y * C
ROW_DEV = 128
CAP = 16
D = 8192
KVW = 1024
QKV = D + 2 * KVW
HALF = R // 2
SLOTS = PEERS * CAP
MESH = pl.DeviceIdType.MESH


def exchange(
    id_row, id_col, hidden, base, shrink, expand_q, expand_kv, out,
    wg, outgoing, incoming, shrink_v, base_v, acc, lat_out, lat_in, lat3,
    local_sem, p_send, p_recv, l_send, l_recv, w_recv, z_send, y_send, x_send, c_send,
):
    x = lax.axis_index("group")
    me = lax.axis_index("adapter")
    z, y, c = me // 4, (me // 2) % 2, me % 2

    def index(zz, yy, cc):
        return zz * 4 + yy * 2 + cc

    own_rows = pl.ds(pl.multiple_of(me * R, R), R)
    loads = [
        pltpu.make_async_copy(expand_q.at[0], wg.at[own_rows, 0:D], local_sem.at[0]),
        pltpu.make_async_copy(expand_kv.at[0, 0], wg.at[own_rows, D : D + KVW], local_sem.at[1]),
        pltpu.make_async_copy(expand_kv.at[0, 1], wg.at[own_rows, D + KVW : QKV], local_sem.at[2]),
        pltpu.make_async_copy(shrink.at[0], shrink_v, local_sem.at[3]),
        pltpu.make_async_copy(base, base_v, local_sem.at[4]),
    ]
    for load in loads:
        load.start()

    barrier = pltpu.get_barrier_semaphore()
    for k in range(1, PEERS):
        pl.semaphore_signal(barrier, inc=1, device_id=(x, (me + k) % PEERS), device_id_type=MESH)
    pl.semaphore_signal(barrier, inc=1, device_id=(1 - x, me), device_id_type=MESH)
    pl.semaphore_wait(barrier, PEERS)

    def piece(a, h):
        return wg.at[pl.ds(pl.multiple_of(a * R + h * HALF, HALF), HALF), :]

    def push(a, h, target, sem):
        return pltpu.make_async_remote_copy(
            src_ref=piece(a, h), dst_ref=piece(a, h), send_sem=sem, recv_sem=w_recv.at[a, h],
            device_id=target, device_id_type=MESH,
        )

    def to_up(zz):
        return push(index(zz, y, c), x, (x, index(z + 1, y, c)), z_send.at[zz, 0])

    def to_down(zz):
        return push(index(zz, y, c), x, (x, index(z - 1, y, c)), z_send.at[zz, 1])

    def to_y(zz):
        return push(index(zz, y, c), x, (x, index(z, 1 - y, c)), y_send.at[zz])

    def to_x(zz, yy):
        return push(index(zz, yy, c), x, (1 - x, me), x_send.at[zz, yy])

    def to_core(zz, yy, h):
        return push(index(zz, yy, c), h, (x, index(z, y, 1 - c)), c_send.at[zz, yy, h])

    def arrived(a, h):
        push(a, h, (x, me), c_send.at[0, 0, 0]).wait_recv()

    for load in loads[0:3]:
        load.wait()

    @pl.when(z < Z - 1)
    def _():
        to_up(z).start()

    @pl.when(z > 0)
    def _():
        to_down(z).start()

    to_y(z).start()
    to_core(z, y, 0).start()
    to_core(z, y, 1).start()

    ids_row, ids_col = id_row[...], id_col[...]
    matches = ids_col == ids_row
    first = lax.broadcasted_iota(jnp.int32, (ROW_DEV, ROW_DEV), 0)
    second = lax.broadcasted_iota(jnp.int32, (ROW_DEV, ROW_DEV), 1)
    rank_row = jnp.sum(jnp.where(matches & (first < second), 1, 0), axis=0, keepdims=True)
    rank_col = jnp.sum(jnp.where(matches & (second < first), 1, 0), axis=1, keepdims=True)
    slot_row, slot_col = ids_row * CAP + rank_row, ids_col * CAP + rank_col
    placer = jnp.where(
        lax.broadcasted_iota(jnp.int32, (SLOTS, ROW_DEV), 0) == slot_row, 1.0, 0.0
    ).astype(jnp.bfloat16)
    taker = jnp.where(
        lax.broadcasted_iota(jnp.int32, (ROW_DEV, SLOTS), 1) == slot_col, 1.0, 0.0
    ).astype(jnp.bfloat16)

    @pl.loop(0, D // 1024)
    def _(step):
        columns = pl.ds(pl.multiple_of(step * 1024, 1024), 1024)
        outgoing[:, columns] = jnp.dot(
            placer, hidden[:, columns], preferred_element_type=jnp.float32
        ).astype(jnp.bfloat16)

    def block(ref, device):
        return ref.at[pl.ds(pl.multiple_of(device * CAP, CAP), CAP), :]

    def row_copy(k):
        peer = (me + k) % PEERS
        return pltpu.make_async_remote_copy(
            src_ref=block(outgoing, peer), dst_ref=block(incoming, me),
            send_sem=p_send.at[k], recv_sem=p_recv.at[k], device_id=(x, peer), device_id_type=MESH,
        )

    def latent_copy(k):
        peer = (me + k) % PEERS
        return pltpu.make_async_remote_copy(
            src_ref=block(lat_out, peer), dst_ref=block(lat_in, me),
            send_sem=l_send.at[k], recv_sem=l_recv.at[k], device_id=(x, peer), device_id_type=MESH,
        )

    own = pltpu.make_async_copy(block(outgoing, me), block(incoming, me), local_sem.at[5])
    own.start()
    for k in ORDER:
        row_copy(k).start()

    for distance in range(1, Z):
        for up in (0, 1):
            zz = z - distance if up else z + distance
            inside = zz >= 0 if up else zz < Z
            more = z < Z - 1 if up else z > 0

            @pl.when(inside)
            def _(zz=zz, more=more, up=up):
                arrived(index(zz, y, c), x)

                @pl.when(more)
                def _():
                    (to_up if up else to_down)(zz).start()

                to_y(zz).start()
                to_x(zz, y).start()
                to_core(zz, y, x).start()

    for turn in range(Z):
        zz = (z + turn) % Z
        arrived(index(zz, 1 - y, c), x)
        to_x(zz, 1 - y).start()
        to_core(zz, 1 - y, x).start()

    for turn in range(Z):
        zz = (z + turn) % Z
        for yy in (y, 1 - y):
            if turn == 0 and yy is y:
                continue
            arrived(index(zz, yy, c), 1 - x)
            to_core(zz, yy, 1 - x).start()

    loads[3].wait()
    own.wait()
    for k in range(1, PEERS):
        row_copy(k).wait_recv()

    acc[...] = jnp.zeros_like(acc)

    @pl.loop(0, D // 1024)
    def _(step):
        part = pl.ds(pl.multiple_of(step * 1024, 1024), 1024)
        acc[...] += jnp.dot(incoming[:, part], shrink_v[part, :], preferred_element_type=jnp.float32)

    from_at = lax.broadcasted_iota(jnp.int32, (3 * R, 6 * R), 0)
    to_at = lax.broadcasted_iota(jnp.int32, (3 * R, 6 * R), 1)
    block_of = jnp.where(from_at >= R, 1, 0) + jnp.where(from_at >= 2 * R, 1, 0)
    spread = jnp.where(to_at == from_at + R * block_of + R * c, 1.0, 0.0).astype(jnp.bfloat16)
    lat_out[...] = jnp.dot(
        acc[...].astype(jnp.bfloat16), spread, preferred_element_type=jnp.float32
    ).astype(jnp.bfloat16)

    for k in range(1, PEERS):
        latent_copy(k).start()
    own_slots = pl.ds(pl.multiple_of(me * CAP, CAP), CAP)
    lat_in[own_slots, :] = lat_out[own_slots, :]

    for zz in range(Z):
        for yy in range(Y):
            for h in range(2):
                arrived(index(zz, yy, 1 - c), h)
    loads[4].wait()
    for k in range(1, PEERS):
        latent_copy(k).wait_recv()

    for pair in range(PEERS // 2):
        slots = slice(pair * 2 * CAP, (pair + 1) * 2 * CAP)
        got = jnp.dot(taker[:, slots], lat_in[slots, :], preferred_element_type=jnp.float32).astype(jnp.bfloat16)
        for which in range(3):
            lat3[which, :, pair * 128 : (pair + 1) * 128] = got[:, which * 128 : (which + 1) * 128]

    def finish(which, columns):
        delta = jnp.dot(lat3[which], wg[:, columns], preferred_element_type=jnp.float32).astype(jnp.bfloat16)
        out[:, columns] = (base_v[:, columns].astype(jnp.float32) + delta.astype(jnp.float32)).astype(jnp.bfloat16)

    @pl.loop(0, D // 512)
    def _(step):
        finish(0, pl.ds(pl.multiple_of(step * 512, 512), 512))

    for which in (1, 2):

        @pl.loop(0, KVW // 512)
        def _(step, which=which):
            finish(which, pl.ds(pl.multiple_of(D + (which - 1) * KVW + step * 512, 512), 512))

    for k in range(1, PEERS):
        row_copy(k).wait_send()
        latent_copy(k).wait_send()
    for zz in range(Z):

        @pl.when((z < Z - 1) & (zz <= z))
        def _(zz=zz):
            to_up(zz).wait_send()

        @pl.when((z > 0) & (zz >= z))
        def _(zz=zz):
            to_down(zz).wait_send()

        to_y(zz).wait_send()
        for yy in range(Y):
            for h in range(2):
                to_core(zz, yy, h).wait_send()

            @pl.when((zz != z) | (yy != y))
            def _(zz=zz, yy=yy):
                to_x(zz, yy).wait_send()


ORDER = tuple(range(1, PEERS))


def gathered(hidden, base_qkv, adapter_id, shrink, expand_q, expand_kv):
    dma = pltpu.SemaphoreType.DMA
    vmem, anywhere = pl.BlockSpec(memory_space=pltpu.VMEM), pl.BlockSpec(memory_space=pl.ANY)
    bf16 = jnp.bfloat16
    return pl.pallas_call(
        exchange,
        out_shape=jax.ShapeDtypeStruct((ROW_DEV, QKV), bf16),
        in_specs=[vmem, vmem, vmem, anywhere, anywhere, anywhere, anywhere],
        out_specs=vmem,
        scratch_shapes=[
            pltpu.VMEM((PEERS * R, QKV), bf16),
            pltpu.VMEM((SLOTS, D), bf16),
            pltpu.VMEM((SLOTS, D), bf16),
            pltpu.VMEM((D, 3 * R), bf16),
            pltpu.VMEM((ROW_DEV, QKV), bf16),
            pltpu.VMEM((SLOTS, 3 * R), jnp.float32),
            pltpu.VMEM((SLOTS, 6 * R), bf16),
            pltpu.VMEM((SLOTS, 6 * R), bf16),
            pltpu.VMEM((3, ROW_DEV, PEERS * R), bf16),
            dma((6,)),
            dma((PEERS,)),
            dma((PEERS,)),
            dma((PEERS,)),
            dma((PEERS,)),
            dma((PEERS, 2)),
            dma((Z, 2)),
            dma((Z,)),
            dma((Z, Y)),
            dma((Z, Y, 2)),
        ],
        compiler_params=pltpu.CompilerParams(
            collective_id=0, has_side_effects=True, vmem_limit_bytes=56 * 1024 * 1024
        ),
        cost_estimate=pl.CostEstimate(flops=4 * 10**9, bytes_accessed=12 * 10**6, transcendentals=0),
    )(adapter_id.reshape(1, ROW_DEV), adapter_id, hidden, base_qkv, shrink, expand_q, expand_kv)


def fits(mesh, hidden, shrink, expand_q):
    groups, peers = mesh.shape["group"], mesh.shape["adapter"]
    return (
        (groups, peers) == (2, PEERS)
        and hidden.shape == (groups * peers * ROW_DEV, D)
        and shrink.shape == (PEERS, D, 3 * R)
        and expand_q.shape == (PEERS, R, D)
    )


def solution(mesh):
    placed = (
        P(("group", "adapter"), None),
        P(("group", "adapter"), None),
        P(("group", "adapter"), None),
        P("adapter", None, None),
        P("adapter", None, None),
        P("adapter", None, None, None),
    )

    def whole(hidden, base_qkv, adapter_id, shrink, expand_q, expand_kv):
        body = gathered if fits(mesh, hidden, shrink, expand_q) else per_device
        return mapped(body)(hidden, base_qkv, adapter_id, shrink, expand_q, expand_kv)

    mapped = lambda body: jax.shard_map(
        body,
        mesh=mesh,
        in_specs=placed,
        out_specs=P(("group", "adapter"), None),
        check_vma=False,
    )
    return whole
```

```python
import jax
import jax.numpy as jnp
from jax import lax
from jax.experimental import pallas as pl
from jax.experimental.pallas import tpu as pltpu
from jax.sharding import PartitionSpec as P

R = 64


def project(latent, weight):
    return jnp.einsum("sacr,are->sace", latent, weight, preferred_element_type=jnp.float32).astype(
        jnp.bfloat16
    )


def per_device(hidden, base_qkv, adapter_id, shrink, expand_q, expand_kv):
    peer_count = lax.axis_size("adapter")
    row_count = hidden.shape[0]
    owned_count = shrink.shape[0]
    model_width = hidden.shape[1]
    slot_cap = max(2, (2 * row_count + peer_count * owned_count - 1) // (peer_count * owned_count))
    row_adapter = adapter_id[:, 0]
    matches = (row_adapter[:, None] == row_adapter[None, :]).astype(jnp.int32)
    earlier = lax.broadcasted_iota(jnp.int32, (row_count, row_count), 0) < lax.broadcasted_iota(
        jnp.int32, (row_count, row_count), 1
    )
    rank_in = jnp.sum(matches * earlier.astype(jnp.int32), axis=0)
    slot_of = row_adapter * slot_cap + rank_in
    slot_count = peer_count * owned_count * slot_cap
    placer = (
        lax.broadcasted_iota(jnp.int32, (slot_count, row_count), 0) == slot_of[None, :]
    ).astype(jnp.bfloat16)
    outgoing = jnp.dot(placer, hidden, preferred_element_type=jnp.float32).astype(jnp.bfloat16)
    outgoing = outgoing.reshape(peer_count, owned_count, slot_cap, model_width)
    latent = jnp.einsum(
        "sacd,adr->sacr",
        lax.all_to_all(outgoing, "adapter", split_axis=0, concat_axis=0, tiled=True),
        shrink,
        preferred_element_type=jnp.float32,
    ).astype(jnp.bfloat16)
    query_delta = project(latent[..., 0:R], expand_q)
    key_delta = project(latent[..., R : 2 * R], expand_kv[:, 0])
    value_delta = project(latent[..., 2 * R : 3 * R], expand_kv[:, 1])
    joined = jnp.concatenate([query_delta, key_delta, value_delta], axis=3)
    returned = lax.all_to_all(joined, "adapter", split_axis=0, concat_axis=0, tiled=True)
    flattened = returned.reshape(slot_count, returned.shape[3])
    deltas = jnp.take(flattened, slot_of, axis=0)
    return (base_qkv.astype(jnp.float32) + deltas.astype(jnp.float32)).astype(jnp.bfloat16)


Z, Y, C = 4, 2, 2
PEERS = Z * Y * C
ROW_DEV = 128
CAP = 16
D = 8192
KVW = 1024
QKV = D + 2 * KVW
HALF = R // 2
SLOTS = PEERS * CAP
MESH = pl.DeviceIdType.MESH


def exchange(
    id_row, hidden, base, shrink, expand_q, expand_kv, out,
    wg, outgoing, incoming, shrink_v, base_v, latents, lat_out, lat_in, lat3, total,
    local_sem, p_send, p_recv, l_send, l_recv, w_recv, z_send, y_send, x_send, c_send,
):
    x = lax.axis_index("group")
    me = lax.axis_index("adapter")
    z, y, c = me // 4, (me // 2) % 2, me % 2
    at = me % 4
    planes = (z, z + 1 - 2 * (z % 2), (z + 2) % 4, 3 - z)

    def index(zz, yy, cc):
        return zz * 4 + yy * 2 + cc

    own_rows = pl.ds(pl.multiple_of(me * R, R), R)
    loads = [
        pltpu.make_async_copy(expand_q.at[0], wg.at[own_rows, 0:D], local_sem.at[0]),
        pltpu.make_async_copy(expand_kv.at[0, 0], wg.at[own_rows, D : D + KVW], local_sem.at[1]),
        pltpu.make_async_copy(expand_kv.at[0, 1], wg.at[own_rows, D + KVW : QKV], local_sem.at[2]),
        pltpu.make_async_copy(shrink.at[0], shrink_v, local_sem.at[3]),
        pltpu.make_async_copy(base, base_v, local_sem.at[4]),
    ]
    for load in loads:
        load.start()

    barrier = pltpu.get_barrier_semaphore()
    for k in range(1, PEERS):
        pl.semaphore_signal(barrier, inc=1, device_id=(x, (me + k) % PEERS), device_id_type=MESH)
    pl.semaphore_signal(barrier, inc=1, device_id=(1 - x, me), device_id_type=MESH)
    pl.semaphore_wait(barrier, PEERS)

    def piece(a, h):
        return wg.at[pl.ds(pl.multiple_of(a * R + h * HALF, HALF), HALF), :]

    def push(a, h, target, sem):
        return pltpu.make_async_remote_copy(
            src_ref=piece(a, h), dst_ref=piece(a, h), send_sem=sem, recv_sem=w_recv.at[a, h],
            device_id=target, device_id_type=MESH,
        )

    def to_up(zz):
        return push(index(zz, y, c), x, (x, index(z + 1, y, c)), z_send.at[zz, 0])

    def to_down(zz):
        return push(index(zz, y, c), x, (x, index(z - 1, y, c)), z_send.at[zz, 1])

    def to_y(zz):
        return push(index(zz, y, c), x, (x, index(z, 1 - y, c)), y_send.at[zz])

    def to_x(zz, yy):
        return push(index(zz, yy, c), x, (1 - x, me), x_send.at[zz, yy])

    def to_core(zz, yy, h):
        return push(index(zz, yy, c), h, (x, index(z, y, 1 - c)), c_send.at[zz, yy, h])

    def arrived(a, h):
        push(a, h, (x, me), c_send.at[0, 0, 0]).wait_recv()

    for load in loads[0:3]:
        load.wait()

    @pl.when(z < Z - 1)
    def _():
        to_up(z).start()

    @pl.when(z > 0)
    def _():
        to_down(z).start()

    to_y(z).start()
    to_core(z, y, 0).start()
    to_core(z, y, 1).start()

    first = lax.broadcasted_iota(jnp.int32, (ROW_DEV, ROW_DEV), 0)
    second = lax.broadcasted_iota(jnp.int32, (ROW_DEV, ROW_DEV), 1)
    ids = id_row[...]
    ids_col = jnp.sum(jnp.where(first == second, ids, 0), axis=1, keepdims=True)
    rank = jnp.sum(jnp.where((ids_col == ids) & (first < second), 1, 0), axis=0, keepdims=True)
    plane = sum(jnp.where(ids >= 4 * p, 1, 0) for p in range(1, Z))
    place = sum(jnp.where(plane == planes[g], g, 0) for g in range(1, Z))
    slot = place * (4 * CAP) + (ids - 4 * plane) * CAP + rank
    slot_col = jnp.sum(jnp.where(first == second, slot, 0), axis=1, keepdims=True)
    placer = jnp.where(
        lax.broadcasted_iota(jnp.int32, (SLOTS, ROW_DEV), 0) == slot, 1.0, 0.0
    ).astype(jnp.bfloat16)
    taker = jnp.where(
        lax.broadcasted_iota(jnp.int32, (ROW_DEV, SLOTS), 1) == slot_col, 1.0, 0.0
    ).astype(jnp.bfloat16)
    from_at = lax.broadcasted_iota(jnp.int32, (3 * R, 6 * R), 0)
    to_at = lax.broadcasted_iota(jnp.int32, (3 * R, 6 * R), 1)
    block_of = jnp.where(from_at >= R, 1, 0) + jnp.where(from_at >= 2 * R, 1, 0)
    spread = jnp.where(to_at == from_at + R * block_of + R * c, 1.0, 0.0).astype(jnp.bfloat16)

    @pl.loop(0, D // 1024)
    def _(step):
        columns = pl.ds(pl.multiple_of(step * 1024, 1024), 1024)
        outgoing[:, columns] = jnp.dot(
            placer, hidden[:, columns], preferred_element_type=jnp.float32
        ).astype(jnp.bfloat16)

    def block(ref, g, n):
        return ref.at[pl.ds(pl.multiple_of((g * 4 + n) * CAP, CAP), CAP), :]

    def peer_copy(source, landing, send, recv, g, j):
        n = (at + j) % 2 + (at // 2 + j // 2) % 2 * 2
        return pltpu.make_async_remote_copy(
            src_ref=block(source, g, n), dst_ref=block(landing, g, at),
            send_sem=send.at[g * 4 + j], recv_sem=recv.at[g * 4 + j],
            device_id=(x, planes[g] * 4 + n), device_id_type=MESH,
        )

    def row_copy(g, j):
        return peer_copy(outgoing, incoming, p_send, p_recv, g, j)

    def latent_copy(g, j):
        return peer_copy(lat_out, lat_in, l_send, l_recv, g, j)

    def others(g):
        return [j for j in range(4) if (g, j) != (0, 0)]

    def send_rows(g, near):
        for j in others(g):
            if (j < 2) == near:
                row_copy(g, j).start()

    def serve(g):
        for j in others(g):
            row_copy(g, j).wait_recv()
        span = slice(g * 4 * CAP, (g + 1) * 4 * CAP)
        latents[...] = jnp.zeros_like(latents)

        @pl.loop(0, D // 1024)
        def _(step):
            part = pl.ds(pl.multiple_of(step * 1024, 1024), 1024)
            latents[...] += lax.dot_general(
                incoming[span, part], shrink_v[:, part], (((1,), (1,)), ((), ())),
                preferred_element_type=jnp.float32,
            )

        lat_out[span, :] = jnp.dot(
            latents[...].astype(jnp.bfloat16), spread, preferred_element_type=jnp.float32
        ).astype(jnp.bfloat16)
        for j in others(g):
            latent_copy(g, j).start()
        if g == 0:
            own_slots = pl.ds(pl.multiple_of(at * CAP, CAP), CAP)
            lat_in[own_slots, :] = lat_out[own_slots, :]

    def add_plane(g):
        for yy in range(Y):
            for h in range(2):
                arrived(index(planes[g], yy, 1 - c), h)
        for j in others(g):
            latent_copy(g, j).wait_recv()
        for pair in range(2):
            slots = slice((2 * g + pair) * 2 * CAP, (2 * g + pair + 1) * 2 * CAP)
            got = jnp.dot(taker[:, slots], lat_in[slots, :], preferred_element_type=jnp.float32)
            got = got.astype(jnp.bfloat16)
            for which in range(3):
                lat3[which, :, pair * 128 : (pair + 1) * 128] = got[:, which * 128 : (which + 1) * 128]
        rows = pl.ds(pl.multiple_of(planes[g] * 4 * R, 4 * R), 4 * R)

        def add(which, columns):
            term = jnp.dot(lat3[which], wg[rows, columns], preferred_element_type=jnp.float32)
            if g > 0:
                term += total[:, columns]
            if g < Z - 1:
                total[:, columns] = term
            else:
                delta = term.astype(jnp.bfloat16).astype(jnp.float32)
                out[:, columns] = (base_v[:, columns].astype(jnp.float32) + delta).astype(jnp.bfloat16)

        @pl.loop(0, D // 512)
        def _(step):
            add(0, pl.ds(pl.multiple_of(step * 512, 512), 512))

        for which in (1, 2):

            @pl.loop(0, KVW // 512)
            def _(step):
                add(which, pl.ds(pl.multiple_of(D + (which - 1) * KVW + step * 512, 512), 512))

    def relay_z(distance):
        for up in (0, 1):
            zz = z - distance if up else z + distance
            inside = zz >= 0 if up else zz < Z
            more = z < Z - 1 if up else z > 0

            @pl.when(inside)
            def _(zz=zz, more=more, up=up):
                arrived(index(zz, y, c), x)

                @pl.when(more)
                def _():
                    (to_up if up else to_down)(zz).start()

                to_y(zz).start()
                to_x(zz, y).start()
                to_core(zz, y, x).start()

    def relay_y(g):
        zz = planes[g]
        arrived(index(zz, 1 - y, c), x)
        to_x(zz, 1 - y).start()
        to_core(zz, 1 - y, x).start()

    def relay_x(g):
        zz = planes[g]
        for yy in (1 - y,) if g == 0 else (y, 1 - y):
            arrived(index(zz, yy, c), 1 - x)
            to_core(zz, yy, 1 - x).start()

    own = pltpu.make_async_copy(block(outgoing, 0, at), block(incoming, 0, at), local_sem.at[5])
    own.start()
    relay_z(1)
    relay_z(2)
    send_rows(1, True)
    relay_z(3)
    send_rows(3, True)
    send_rows(2, True)
    send_rows(0, True)
    relay_y(0)
    relay_y(1)
    relay_y(2)
    relay_y(3)
    send_rows(1, False)
    send_rows(0, False)
    send_rows(3, False)
    send_rows(2, False)
    relay_x(0)
    loads[3].wait()
    own.wait()
    serve(0)
    relay_x(1)
    serve(1)
    relay_x(2)
    relay_x(3)
    loads[4].wait()
    add_plane(0)
    add_plane(1)
    serve(2)
    serve(3)
    add_plane(2)
    add_plane(3)
    for g in range(Z):
        for j in others(g):
            row_copy(g, j).wait_send()
            latent_copy(g, j).wait_send()
    for zz in range(Z):

        @pl.when((z < Z - 1) & (zz <= z))
        def _(zz=zz):
            to_up(zz).wait_send()

        @pl.when((z > 0) & (zz >= z))
        def _(zz=zz):
            to_down(zz).wait_send()

        to_y(zz).wait_send()
        for yy in range(Y):
            for h in range(2):
                to_core(zz, yy, h).wait_send()

            @pl.when((zz != z) | (yy != y))
            def _(zz=zz, yy=yy):
                to_x(zz, yy).wait_send()


def gathered(hidden, base_qkv, adapter_id, shrink, expand_q, expand_kv):
    dma = pltpu.SemaphoreType.DMA
    vmem, anywhere = pl.BlockSpec(memory_space=pltpu.VMEM), pl.BlockSpec(memory_space=pl.ANY)
    bf16 = jnp.bfloat16
    return pl.pallas_call(
        exchange,
        out_shape=jax.ShapeDtypeStruct((ROW_DEV, QKV), bf16),
        in_specs=[vmem, vmem, anywhere, anywhere, anywhere, anywhere],
        out_specs=vmem,
        scratch_shapes=[
            pltpu.VMEM((PEERS * R, QKV), bf16),
            pltpu.VMEM((SLOTS, D), bf16),
            pltpu.VMEM((SLOTS, D), bf16),
            pltpu.VMEM((3 * R, D), bf16),
            pltpu.VMEM((ROW_DEV, QKV), bf16),
            pltpu.VMEM((4 * CAP, 3 * R), jnp.float32),
            pltpu.VMEM((SLOTS, 6 * R), bf16),
            pltpu.VMEM((SLOTS, 6 * R), bf16),
            pltpu.VMEM((3, ROW_DEV, 4 * R), bf16),
            pltpu.VMEM((ROW_DEV, QKV), jnp.float32),
            dma((6,)),
            dma((PEERS,)),
            dma((PEERS,)),
            dma((PEERS,)),
            dma((PEERS,)),
            dma((PEERS, 2)),
            dma((Z, 2)),
            dma((Z,)),
            dma((Z, Y)),
            dma((Z, Y, 2)),
        ],
        compiler_params=pltpu.CompilerParams(
            collective_id=0, has_side_effects=True, vmem_limit_bytes=56 * 1024 * 1024
        ),
        cost_estimate=pl.CostEstimate(flops=4 * 10**9, bytes_accessed=12 * 10**6, transcendentals=0),
    )(
        adapter_id.reshape(1, ROW_DEV), hidden, base_qkv, jnp.swapaxes(shrink, 1, 2), expand_q, expand_kv
    )


def fits(mesh, hidden, shrink, expand_q):
    groups, peers = mesh.shape["group"], mesh.shape["adapter"]
    return (
        (groups, peers) == (2, PEERS)
        and hidden.shape == (groups * peers * ROW_DEV, D)
        and shrink.shape == (PEERS, D, 3 * R)
        and expand_q.shape == (PEERS, R, D)
    )


def solution(mesh):
    placed = (
        P(("group", "adapter"), None),
        P(("group", "adapter"), None),
        P(("group", "adapter"), None),
        P("adapter", None, None),
        P("adapter", None, None),
        P("adapter", None, None, None),
    )

    def whole(hidden, base_qkv, adapter_id, shrink, expand_q, expand_kv):
        body = gathered if fits(mesh, hidden, shrink, expand_q) else per_device
        return mapped(body)(hidden, base_qkv, adapter_id, shrink, expand_q, expand_kv)

    mapped = lambda body: jax.shard_map(
        body,
        mesh=mesh,
        in_specs=placed,
        out_specs=P(("group", "adapter"), None),
        check_vma=False,
    )
    return whole
```

```python
import jax
import jax.numpy as jnp
from jax import lax
from jax.experimental import pallas as pl
from jax.experimental.pallas import tpu as pltpu
from jax.sharding import PartitionSpec as P

R = 64


def project(latent, weight):
    return jnp.einsum("sacr,are->sace", latent, weight, preferred_element_type=jnp.float32).astype(
        jnp.bfloat16
    )


def per_device(hidden, base_qkv, adapter_id, shrink, expand_q, expand_kv):
    peer_count = lax.axis_size("adapter")
    row_count = hidden.shape[0]
    owned_count = shrink.shape[0]
    model_width = hidden.shape[1]
    slot_cap = max(2, (2 * row_count + peer_count * owned_count - 1) // (peer_count * owned_count))
    row_adapter = adapter_id[:, 0]
    matches = (row_adapter[:, None] == row_adapter[None, :]).astype(jnp.int32)
    earlier = lax.broadcasted_iota(jnp.int32, (row_count, row_count), 0) < lax.broadcasted_iota(
        jnp.int32, (row_count, row_count), 1
    )
    rank_in = jnp.sum(matches * earlier.astype(jnp.int32), axis=0)
    slot_of = row_adapter * slot_cap + rank_in
    slot_count = peer_count * owned_count * slot_cap
    placer = (
        lax.broadcasted_iota(jnp.int32, (slot_count, row_count), 0) == slot_of[None, :]
    ).astype(jnp.bfloat16)
    outgoing = jnp.dot(placer, hidden, preferred_element_type=jnp.float32).astype(jnp.bfloat16)
    outgoing = outgoing.reshape(peer_count, owned_count, slot_cap, model_width)
    latent = jnp.einsum(
        "sacd,adr->sacr",
        lax.all_to_all(outgoing, "adapter", split_axis=0, concat_axis=0, tiled=True),
        shrink,
        preferred_element_type=jnp.float32,
    ).astype(jnp.bfloat16)
    query_delta = project(latent[..., 0:R], expand_q)
    key_delta = project(latent[..., R : 2 * R], expand_kv[:, 0])
    value_delta = project(latent[..., 2 * R : 3 * R], expand_kv[:, 1])
    joined = jnp.concatenate([query_delta, key_delta, value_delta], axis=3)
    returned = lax.all_to_all(joined, "adapter", split_axis=0, concat_axis=0, tiled=True)
    flattened = returned.reshape(slot_count, returned.shape[3])
    deltas = jnp.take(flattened, slot_of, axis=0)
    return (base_qkv.astype(jnp.float32) + deltas.astype(jnp.float32)).astype(jnp.bfloat16)


Z, Y, C = 4, 2, 2
PEERS = Z * Y * C
ROW_DEV = 128
CAP = 16
D = 8192
KVW = 1024
QKV = D + 2 * KVW
HALF = R // 2
WIDE = 1024
SLOTS = PEERS * CAP
MESH = pl.DeviceIdType.MESH


def exchange(
    id_row, hidden, base, shrink, expand_q, expand_kv, out,
    wg, outgoing, incoming, shrink_v, base_v, latents, lat_out, lat_in, lat3, total,
    local_sem, p_send, p_recv, l_send, l_recv, w_recv, z_send, y_send, x_send, c_send,
):
    x = lax.axis_index("group")
    me = lax.axis_index("adapter")
    z, y, c = me // 4, (me // 2) % 2, me % 2
    at = me % 4
    planes = (z, z + 1 - 2 * (z % 2), (z + 2) % 4, 3 - z)

    def index(zz, yy, cc):
        return zz * 4 + yy * 2 + cc

    own_rows = pl.ds(pl.multiple_of(me * R, R), R)
    loads = [
        pltpu.make_async_copy(expand_q.at[0], wg.at[own_rows, 0:D], local_sem.at[0]),
        pltpu.make_async_copy(expand_kv.at[0, 0], wg.at[own_rows, D : D + KVW], local_sem.at[1]),
        pltpu.make_async_copy(expand_kv.at[0, 1], wg.at[own_rows, D + KVW : QKV], local_sem.at[2]),
        pltpu.make_async_copy(shrink.at[0], shrink_v, local_sem.at[3]),
        pltpu.make_async_copy(base, base_v, local_sem.at[4]),
    ]
    for load in loads:
        load.start()

    barrier = pltpu.get_barrier_semaphore()
    for k in range(1, PEERS):
        pl.semaphore_signal(barrier, inc=1, device_id=(x, (me + k) % PEERS), device_id_type=MESH)
    pl.semaphore_signal(barrier, inc=1, device_id=(1 - x, me), device_id_type=MESH)
    pl.semaphore_wait(barrier, PEERS)

    def piece(a, h):
        return wg.at[pl.ds(pl.multiple_of(a * R + h * HALF, HALF), HALF), :]

    def push(a, h, target, sem):
        return pltpu.make_async_remote_copy(
            src_ref=piece(a, h), dst_ref=piece(a, h), send_sem=sem, recv_sem=w_recv.at[a, h],
            device_id=target, device_id_type=MESH,
        )

    def to_up(zz):
        return push(index(zz, y, c), x, (x, index(z + 1, y, c)), z_send.at[zz, 0])

    def to_down(zz):
        return push(index(zz, y, c), x, (x, index(z - 1, y, c)), z_send.at[zz, 1])

    def to_y(zz):
        return push(index(zz, y, c), x, (x, index(z, 1 - y, c)), y_send.at[zz])

    def to_x(zz, yy):
        return push(index(zz, yy, c), x, (1 - x, me), x_send.at[zz, yy])

    def to_core(zz, yy, h):
        return push(index(zz, yy, c), h, (x, index(z, y, 1 - c)), c_send.at[zz, yy, h])

    def arrived(a, h):
        push(a, h, (x, me), c_send.at[0, 0, 0]).wait_recv()

    for load in loads[0:3]:
        load.wait()

    @pl.when(z < Z - 1)
    def _():
        to_up(z).start()

    @pl.when(z > 0)
    def _():
        to_down(z).start()

    to_y(z).start()
    to_core(z, y, 0).start()
    to_core(z, y, 1).start()

    first = lax.broadcasted_iota(jnp.int32, (ROW_DEV, ROW_DEV), 0)
    second = lax.broadcasted_iota(jnp.int32, (ROW_DEV, ROW_DEV), 1)
    ids = id_row[...]
    ids_col = jnp.sum(jnp.where(first == second, ids, 0), axis=1, keepdims=True)
    rank = jnp.sum(jnp.where((ids_col == ids) & (first < second), 1, 0), axis=0, keepdims=True)
    plane = sum(jnp.where(ids >= 4 * p, 1, 0) for p in range(1, Z))
    place = sum(jnp.where(plane == planes[g], g, 0) for g in range(1, Z))
    slot = place * (4 * CAP) + (ids - 4 * plane) * CAP + rank
    slot_col = jnp.sum(jnp.where(first == second, slot, 0), axis=1, keepdims=True)
    placer = jnp.where(
        lax.broadcasted_iota(jnp.int32, (SLOTS, ROW_DEV), 0) == slot, 1.0, 0.0
    ).astype(jnp.bfloat16)
    taker = jnp.where(
        lax.broadcasted_iota(jnp.int32, (ROW_DEV, SLOTS), 1) == slot_col, 1.0, 0.0
    ).astype(jnp.bfloat16)
    from_at = lax.broadcasted_iota(jnp.int32, (3 * R, 6 * R), 0)
    to_at = lax.broadcasted_iota(jnp.int32, (3 * R, 6 * R), 1)
    block_of = jnp.where(from_at >= R, 1, 0) + jnp.where(from_at >= 2 * R, 1, 0)
    spread = jnp.where(to_at == from_at + R * block_of + R * c, 1.0, 0.0).astype(jnp.bfloat16)

    @pl.loop(0, D // 1024)
    def _(step):
        columns = pl.ds(pl.multiple_of(step * 1024, 1024), 1024)
        outgoing[:, columns] = jnp.dot(
            placer, hidden[:, columns], preferred_element_type=jnp.float32
        ).astype(jnp.bfloat16)

    def block(ref, g, n):
        return ref.at[pl.ds(pl.multiple_of((g * 4 + n) * CAP, CAP), CAP), :]

    def peer_copy(source, landing, send, recv, g, j):
        n = (at + j) % 2 + (at // 2 + j // 2) % 2 * 2
        return pltpu.make_async_remote_copy(
            src_ref=block(source, g, n), dst_ref=block(landing, g, at),
            send_sem=send.at[g * 4 + j], recv_sem=recv.at[g * 4 + j],
            device_id=(x, planes[g] * 4 + n), device_id_type=MESH,
        )

    def row_copy(g, j):
        return peer_copy(outgoing, incoming, p_send, p_recv, g, j)

    def latent_copy(g, j):
        return peer_copy(lat_out, lat_in, l_send, l_recv, g, j)

    def others(g):
        return [j for j in range(4) if (g, j) != (0, 0)]

    def send_rows(g, near):
        for j in others(g):
            if (j < 2) == near:
                row_copy(g, j).start()

    def serve(*pair):
        for g in pair:
            for j in others(g):
                row_copy(g, j).wait_recv()
        span = slice(pair[0] * 4 * CAP, (pair[-1] + 1) * 4 * CAP)
        latents[...] = jnp.zeros_like(latents)

        @pl.loop(0, D // 2048)
        def _(step):
            part = pl.ds(pl.multiple_of(step * 2048, 2048), 2048)
            latents[...] += lax.dot_general(
                incoming[span, part], shrink_v[:, part], (((1,), (1,)), ((), ())),
                preferred_element_type=jnp.float32,
            )

        lat_out[span, :] = jnp.dot(
            latents[...].astype(jnp.bfloat16), spread, preferred_element_type=jnp.float32
        ).astype(jnp.bfloat16)
        for g in pair:
            for j in others(g):
                latent_copy(g, j).start()
        if pair[0] == 0:
            own_slots = pl.ds(pl.multiple_of(at * CAP, CAP), CAP)
            lat_in[own_slots, :] = lat_out[own_slots, :]

    def add_planes(*pair):
        for g in pair:
            for yy in range(Y):
                for h in range(2):
                    arrived(index(planes[g], yy, 1 - c), h)
        for g in pair:
            for j in others(g):
                latent_copy(g, j).wait_recv()
            for two in range(2):
                slots = slice((2 * g + two) * 2 * CAP, (2 * g + two + 1) * 2 * CAP)
                got = jnp.dot(taker[:, slots], lat_in[slots, :], preferred_element_type=jnp.float32)
                got = got.astype(jnp.bfloat16)
                lane = (g - pair[0]) * 256 + two * 128
                for which in range(3):
                    lat3[which, :, lane : lane + 128] = got[:, which * 128 : (which + 1) * 128]

        def add(which, columns):
            term = None
            for i, g in enumerate(pair):
                rows = pl.ds(pl.multiple_of(planes[g] * 4 * R, 4 * R), 4 * R)
                product = jnp.dot(
                    lat3[which, :, i * 256 : (i + 1) * 256], wg[rows, columns],
                    preferred_element_type=jnp.float32,
                )
                term = product if term is None else term + product
            if pair[0] > 0:
                term += total[:, columns]
            if pair[-1] < Z - 1:
                total[:, columns] = term
            else:
                delta = term.astype(jnp.bfloat16).astype(jnp.float32)
                out[:, columns] = (base_v[:, columns].astype(jnp.float32) + delta).astype(jnp.bfloat16)

        @pl.loop(0, D // WIDE)
        def _(step):
            add(0, pl.ds(pl.multiple_of(step * WIDE, WIDE), WIDE))

        add(1, slice(D, D + KVW))
        add(2, slice(D + KVW, QKV))

    def relay_z(distance):
        for up in (0, 1):
            zz = z - distance if up else z + distance
            inside = zz >= 0 if up else zz < Z
            more = z < Z - 1 if up else z > 0

            @pl.when(inside)
            def _(zz=zz, more=more, up=up):
                arrived(index(zz, y, c), x)

                @pl.when(more)
                def _():
                    (to_up if up else to_down)(zz).start()

                to_y(zz).start()
                to_x(zz, y).start()
                to_core(zz, y, x).start()

    def relay_y(g):
        zz = planes[g]
        arrived(index(zz, 1 - y, c), x)
        to_x(zz, 1 - y).start()
        to_core(zz, 1 - y, x).start()

    def relay_x(g):
        zz = planes[g]
        for yy in (1 - y,) if g == 0 else (y, 1 - y):
            arrived(index(zz, yy, c), 1 - x)
            to_core(zz, yy, 1 - x).start()

    own = pltpu.make_async_copy(block(outgoing, 0, at), block(incoming, 0, at), local_sem.at[5])
    own.start()
    relay_z(1)
    relay_z(2)
    send_rows(1, True)
    relay_z(3)
    send_rows(3, True)
    send_rows(2, True)
    send_rows(0, True)
    relay_y(0)
    relay_y(1)
    relay_y(2)
    relay_y(3)
    send_rows(1, False)
    send_rows(0, False)
    send_rows(3, False)
    send_rows(2, False)
    relay_x(0)
    loads[3].wait()
    own.wait()
    serve(0, 1)
    relay_x(1)
    loads[4].wait()
    add_planes(0, 1)
    relay_x(2)
    relay_x(3)
    serve(2, 3)
    add_planes(2, 3)
    for g in range(Z):
        for j in others(g):
            row_copy(g, j).wait_send()
            latent_copy(g, j).wait_send()
    for zz in range(Z):

        @pl.when((z < Z - 1) & (zz <= z))
        def _(zz=zz):
            to_up(zz).wait_send()

        @pl.when((z > 0) & (zz >= z))
        def _(zz=zz):
            to_down(zz).wait_send()

        to_y(zz).wait_send()
        for yy in range(Y):
            for h in range(2):
                to_core(zz, yy, h).wait_send()

            @pl.when((zz != z) | (yy != y))
            def _(zz=zz, yy=yy):
                to_x(zz, yy).wait_send()


def gathered(hidden, base_qkv, adapter_id, shrink, expand_q, expand_kv):
    dma = pltpu.SemaphoreType.DMA
    vmem, anywhere = pl.BlockSpec(memory_space=pltpu.VMEM), pl.BlockSpec(memory_space=pl.ANY)
    bf16 = jnp.bfloat16
    return pl.pallas_call(
        exchange,
        out_shape=jax.ShapeDtypeStruct((ROW_DEV, QKV), bf16),
        in_specs=[vmem, vmem, anywhere, anywhere, anywhere, anywhere],
        out_specs=vmem,
        scratch_shapes=[
            pltpu.VMEM((PEERS * R, QKV), bf16),
            pltpu.VMEM((SLOTS, D), bf16),
            pltpu.VMEM((SLOTS, D), bf16),
            pltpu.VMEM((3 * R, D), bf16),
            pltpu.VMEM((ROW_DEV, QKV), bf16),
            pltpu.VMEM((8 * CAP, 3 * R), jnp.float32),
            pltpu.VMEM((SLOTS, 6 * R), bf16),
            pltpu.VMEM((SLOTS, 6 * R), bf16),
            pltpu.VMEM((3, ROW_DEV, PEERS * R), bf16),
            pltpu.VMEM((ROW_DEV, QKV), jnp.float32),
            dma((6,)),
            dma((PEERS,)),
            dma((PEERS,)),
            dma((PEERS,)),
            dma((PEERS,)),
            dma((PEERS, 2)),
            dma((Z, 2)),
            dma((Z,)),
            dma((Z, Y)),
            dma((Z, Y, 2)),
        ],
        compiler_params=pltpu.CompilerParams(
            collective_id=0, has_side_effects=True, vmem_limit_bytes=56 * 1024 * 1024
        ),
        cost_estimate=pl.CostEstimate(flops=4 * 10**9, bytes_accessed=12 * 10**6, transcendentals=0),
    )(
        adapter_id.reshape(1, ROW_DEV), hidden, base_qkv, jnp.swapaxes(shrink, 1, 2), expand_q, expand_kv
    )


def fits(mesh, hidden, shrink, expand_q):
    groups, peers = mesh.shape["group"], mesh.shape["adapter"]
    return (
        (groups, peers) == (2, PEERS)
        and hidden.shape == (groups * peers * ROW_DEV, D)
        and shrink.shape == (PEERS, D, 3 * R)
        and expand_q.shape == (PEERS, R, D)
    )


def solution(mesh):
    placed = (
        P(("group", "adapter"), None),
        P(("group", "adapter"), None),
        P(("group", "adapter"), None),
        P("adapter", None, None),
        P("adapter", None, None),
        P("adapter", None, None, None),
    )

    def whole(hidden, base_qkv, adapter_id, shrink, expand_q, expand_kv):
        body = gathered if fits(mesh, hidden, shrink, expand_q) else per_device
        return mapped(body)(hidden, base_qkv, adapter_id, shrink, expand_q, expand_kv)

    mapped = lambda body: jax.shard_map(
        body,
        mesh=mesh,
        in_specs=placed,
        out_specs=P(("group", "adapter"), None),
        check_vma=False,
    )
    return whole
```

```python
import jax
import jax.numpy as jnp
from jax import lax
from jax.experimental import pallas as pl
from jax.experimental.pallas import tpu as pltpu
from jax.sharding import PartitionSpec as P

R = 64


def project(latent, weight):
    return jnp.einsum("sacr,are->sace", latent, weight, preferred_element_type=jnp.float32).astype(
        jnp.bfloat16
    )


def per_device(hidden, base_qkv, adapter_id, shrink, expand_q, expand_kv):
    peer_count = lax.axis_size("adapter")
    row_count = hidden.shape[0]
    owned_count = shrink.shape[0]
    model_width = hidden.shape[1]
    slot_cap = max(2, (2 * row_count + peer_count * owned_count - 1) // (peer_count * owned_count))
    row_adapter = adapter_id[:, 0]
    matches = (row_adapter[:, None] == row_adapter[None, :]).astype(jnp.int32)
    earlier = lax.broadcasted_iota(jnp.int32, (row_count, row_count), 0) < lax.broadcasted_iota(
        jnp.int32, (row_count, row_count), 1
    )
    rank_in = jnp.sum(matches * earlier.astype(jnp.int32), axis=0)
    slot_of = row_adapter * slot_cap + rank_in
    slot_count = peer_count * owned_count * slot_cap
    placer = (
        lax.broadcasted_iota(jnp.int32, (slot_count, row_count), 0) == slot_of[None, :]
    ).astype(jnp.bfloat16)
    outgoing = jnp.dot(placer, hidden, preferred_element_type=jnp.float32).astype(jnp.bfloat16)
    outgoing = outgoing.reshape(peer_count, owned_count, slot_cap, model_width)
    latent = jnp.einsum(
        "sacd,adr->sacr",
        lax.all_to_all(outgoing, "adapter", split_axis=0, concat_axis=0, tiled=True),
        shrink,
        preferred_element_type=jnp.float32,
    ).astype(jnp.bfloat16)
    query_delta = project(latent[..., 0:R], expand_q)
    key_delta = project(latent[..., R : 2 * R], expand_kv[:, 0])
    value_delta = project(latent[..., 2 * R : 3 * R], expand_kv[:, 1])
    joined = jnp.concatenate([query_delta, key_delta, value_delta], axis=3)
    returned = lax.all_to_all(joined, "adapter", split_axis=0, concat_axis=0, tiled=True)
    flattened = returned.reshape(slot_count, returned.shape[3])
    deltas = jnp.take(flattened, slot_of, axis=0)
    return (base_qkv.astype(jnp.float32) + deltas.astype(jnp.float32)).astype(jnp.bfloat16)


Z, Y, C = 4, 2, 2
PEERS = Z * Y * C
ROW_DEV = 128
CAP = 16
D = 8192
KVW = 1024
QKV = D + 2 * KVW
HALF = R // 2
WIDE = 1024
SLOTS = PEERS * CAP
MESH = pl.DeviceIdType.MESH


def exchange(
    id_row, hidden_in, base, shrink, expand_q, expand_kv, result,
    wg, outgoing, incoming, shrink_v, base_v, latents, lat_out, lat_in, lat3, total, hidden, out,
    local_sem, p_send, p_recv, l_send, l_recv, w_recv, z_send, y_send, x_send, c_send, out_sem,
):
    x = lax.axis_index("group")
    me = lax.axis_index("adapter")
    z, y, c = me // 4, (me // 2) % 2, me % 2
    at = me % 4
    planes = (z, z + 1 - 2 * (z % 2), (z + 2) % 4, 3 - z)

    def index(zz, yy, cc):
        return zz * 4 + yy * 2 + cc

    own_rows = pl.ds(pl.multiple_of(me * R, R), R)
    loads = [
        pltpu.make_async_copy(expand_q.at[0], wg.at[own_rows, 0:D], local_sem.at[0]),
        pltpu.make_async_copy(expand_kv.at[0, 0], wg.at[own_rows, D : D + KVW], local_sem.at[1]),
        pltpu.make_async_copy(expand_kv.at[0, 1], wg.at[own_rows, D + KVW : QKV], local_sem.at[2]),
        pltpu.make_async_copy(shrink.at[0], shrink_v, local_sem.at[3]),
        pltpu.make_async_copy(base, base_v, local_sem.at[4]),
        pltpu.make_async_copy(hidden_in, hidden, local_sem.at[6]),
    ]
    for load in loads:
        load.start()

    barrier = pltpu.get_barrier_semaphore()
    for k in range(1, PEERS):
        pl.semaphore_signal(barrier, inc=1, device_id=(x, (me + k) % PEERS), device_id_type=MESH)
    pl.semaphore_signal(barrier, inc=1, device_id=(1 - x, me), device_id_type=MESH)
    pl.semaphore_wait(barrier, PEERS)

    def piece(a, h):
        return wg.at[pl.ds(pl.multiple_of(a * R + h * HALF, HALF), HALF), :]

    def push(a, h, target, sem):
        return pltpu.make_async_remote_copy(
            src_ref=piece(a, h), dst_ref=piece(a, h), send_sem=sem, recv_sem=w_recv.at[a, h],
            device_id=target, device_id_type=MESH,
        )

    def to_up(zz):
        return push(index(zz, y, c), x, (x, index(z + 1, y, c)), z_send.at[zz, 0])

    def to_down(zz):
        return push(index(zz, y, c), x, (x, index(z - 1, y, c)), z_send.at[zz, 1])

    def to_y(zz):
        return push(index(zz, y, c), x, (x, index(z, 1 - y, c)), y_send.at[zz])

    def to_x(zz, yy):
        return push(index(zz, yy, c), x, (1 - x, me), x_send.at[zz, yy])

    def to_core(zz, yy, h):
        return push(index(zz, yy, c), h, (x, index(z, y, 1 - c)), c_send.at[zz, yy, h])

    def arrived(a, h):
        push(a, h, (x, me), c_send.at[0, 0, 0]).wait_recv()

    for load in loads[0:3]:
        load.wait()

    @pl.when(z < Z - 1)
    def _():
        to_up(z).start()

    @pl.when(z > 0)
    def _():
        to_down(z).start()

    to_y(z).start()
    to_core(z, y, 0).start()
    to_core(z, y, 1).start()

    first = lax.broadcasted_iota(jnp.int32, (ROW_DEV, ROW_DEV), 0)
    second = lax.broadcasted_iota(jnp.int32, (ROW_DEV, ROW_DEV), 1)
    ids = id_row[...]
    ids_col = jnp.sum(jnp.where(first == second, ids, 0), axis=1, keepdims=True)
    rank = jnp.sum(jnp.where((ids_col == ids) & (first < second), 1, 0), axis=0, keepdims=True)
    plane = sum(jnp.where(ids >= 4 * p, 1, 0) for p in range(1, Z))
    place = sum(jnp.where(plane == planes[g], g, 0) for g in range(1, Z))
    slot = place * (4 * CAP) + (ids - 4 * plane) * CAP + rank
    slot_col = jnp.sum(jnp.where(first == second, slot, 0), axis=1, keepdims=True)
    placer = jnp.where(
        lax.broadcasted_iota(jnp.int32, (SLOTS, ROW_DEV), 0) == slot, 1.0, 0.0
    ).astype(jnp.bfloat16)
    taker = jnp.where(
        lax.broadcasted_iota(jnp.int32, (ROW_DEV, SLOTS), 1) == slot_col, 1.0, 0.0
    ).astype(jnp.bfloat16)
    from_at = lax.broadcasted_iota(jnp.int32, (3 * R, 6 * R), 0)
    to_at = lax.broadcasted_iota(jnp.int32, (3 * R, 6 * R), 1)
    block_of = jnp.where(from_at >= R, 1, 0) + jnp.where(from_at >= 2 * R, 1, 0)
    spread = jnp.where(to_at == from_at + R * block_of + R * c, 1.0, 0.0).astype(jnp.bfloat16)

    loads[5].wait()

    @pl.loop(0, D // 1024)
    def _(step):
        columns = pl.ds(pl.multiple_of(step * 1024, 1024), 1024)
        outgoing[:, columns] = jnp.dot(
            placer, hidden[:, columns], preferred_element_type=jnp.float32
        ).astype(jnp.bfloat16)

    def block(ref, g, n):
        return ref.at[pl.ds(pl.multiple_of((g * 4 + n) * CAP, CAP), CAP), :]

    def peer_copy(source, landing, send, recv, g, j):
        n = (at + j) % 2 + (at // 2 + j // 2) % 2 * 2
        return pltpu.make_async_remote_copy(
            src_ref=block(source, g, n), dst_ref=block(landing, g, at),
            send_sem=send.at[g * 4 + j], recv_sem=recv.at[g * 4 + j],
            device_id=(x, planes[g] * 4 + n), device_id_type=MESH,
        )

    def row_copy(g, j):
        return peer_copy(outgoing, incoming, p_send, p_recv, g, j)

    def latent_copy(g, j):
        return peer_copy(lat_out, lat_in, l_send, l_recv, g, j)

    def others(g):
        return [j for j in range(4) if (g, j) != (0, 0)]

    def send_rows(g, near):
        for j in others(g):
            if (j < 2) == near:
                row_copy(g, j).start()

    def serve(*pair):
        for g in pair:
            for j in others(g):
                row_copy(g, j).wait_recv()
        span = slice(pair[0] * 4 * CAP, (pair[-1] + 1) * 4 * CAP)
        latents[...] = jnp.zeros_like(latents)

        @pl.loop(0, D // 2048)
        def _(step):
            part = pl.ds(pl.multiple_of(step * 2048, 2048), 2048)
            latents[...] += lax.dot_general(
                incoming[span, part], shrink_v[:, part], (((1,), (1,)), ((), ())),
                preferred_element_type=jnp.float32,
            )

        lat_out[span, :] = jnp.dot(
            latents[...].astype(jnp.bfloat16), spread, preferred_element_type=jnp.float32
        ).astype(jnp.bfloat16)
        for g in pair:
            for j in others(g):
                latent_copy(g, j).start()
        if pair[0] == 0:
            own_slots = pl.ds(pl.multiple_of(at * CAP, CAP), CAP)
            lat_in[own_slots, :] = lat_out[own_slots, :]

    def store(step):
        columns = pl.ds(pl.multiple_of(step * WIDE, WIDE), WIDE)
        return pltpu.make_async_copy(out.at[:, columns], result.at[:, columns], out_sem.at[step])

    def add_planes(*pair):
        for g in pair:
            for yy in range(Y):
                for h in range(2):
                    arrived(index(planes[g], yy, 1 - c), h)
        for g in pair:
            for j in others(g):
                latent_copy(g, j).wait_recv()
            for two in range(2):
                slots = slice((2 * g + two) * 2 * CAP, (2 * g + two + 1) * 2 * CAP)
                got = jnp.dot(taker[:, slots], lat_in[slots, :], preferred_element_type=jnp.float32)
                got = got.astype(jnp.bfloat16)
                lane = (g - pair[0]) * 256 + two * 128
                for which in range(3):
                    lat3[which, :, lane : lane + 128] = got[:, which * 128 : (which + 1) * 128]

        def add(which, columns):
            term = None
            for i, g in enumerate(pair):
                rows = pl.ds(pl.multiple_of(planes[g] * 4 * R, 4 * R), 4 * R)
                product = jnp.dot(
                    lat3[which, :, i * 256 : (i + 1) * 256], wg[rows, columns],
                    preferred_element_type=jnp.float32,
                )
                term = product if term is None else term + product
            if pair[0] > 0:
                term += total[:, columns]
            if pair[-1] < Z - 1:
                total[:, columns] = term
            else:
                delta = term.astype(jnp.bfloat16).astype(jnp.float32)
                out[:, columns] = (base_v[:, columns].astype(jnp.float32) + delta).astype(jnp.bfloat16)

        @pl.loop(0, D // WIDE)
        def _(step):
            add(0, pl.ds(pl.multiple_of(step * WIDE, WIDE), WIDE))
            if pair[-1] == Z - 1:
                store(step).start()

        add(1, slice(D, D + KVW))
        add(2, slice(D + KVW, QKV))
        if pair[-1] == Z - 1:
            for step in range(D // WIDE, QKV // WIDE):
                store(step).start()

    def relay_z(distance):
        for up in (0, 1):
            zz = z - distance if up else z + distance
            inside = zz >= 0 if up else zz < Z
            more = z < Z - 1 if up else z > 0

            @pl.when(inside)
            def _(zz=zz, more=more, up=up):
                arrived(index(zz, y, c), x)

                @pl.when(more)
                def _():
                    (to_up if up else to_down)(zz).start()

                to_y(zz).start()
                to_x(zz, y).start()
                to_core(zz, y, x).start()

    def relay_y(g):
        zz = planes[g]
        arrived(index(zz, 1 - y, c), x)
        to_x(zz, 1 - y).start()
        to_core(zz, 1 - y, x).start()

    def relay_x(g):
        zz = planes[g]
        for yy in (1 - y,) if g == 0 else (y, 1 - y):
            arrived(index(zz, yy, c), 1 - x)
            to_core(zz, yy, 1 - x).start()

    own = pltpu.make_async_copy(block(outgoing, 0, at), block(incoming, 0, at), local_sem.at[5])
    own.start()
    relay_z(1)
    relay_z(2)
    send_rows(1, True)
    relay_z(3)
    send_rows(3, True)
    send_rows(2, True)
    send_rows(0, True)
    relay_y(0)
    relay_y(1)
    relay_y(2)
    relay_y(3)
    send_rows(1, False)
    send_rows(0, False)
    send_rows(3, False)
    send_rows(2, False)
    relay_x(0)
    loads[3].wait()
    own.wait()
    serve(0, 1)
    relay_x(1)
    loads[4].wait()
    add_planes(0, 1)
    relay_x(2)
    relay_x(3)
    serve(2, 3)
    add_planes(2, 3)
    for step in range(QKV // WIDE):
        store(step).wait()
    for g in range(Z):
        for j in others(g):
            row_copy(g, j).wait_send()
            latent_copy(g, j).wait_send()
    for zz in range(Z):

        @pl.when((z < Z - 1) & (zz <= z))
        def _(zz=zz):
            to_up(zz).wait_send()

        @pl.when((z > 0) & (zz >= z))
        def _(zz=zz):
            to_down(zz).wait_send()

        to_y(zz).wait_send()
        for yy in range(Y):
            for h in range(2):
                to_core(zz, yy, h).wait_send()

            @pl.when((zz != z) | (yy != y))
            def _(zz=zz, yy=yy):
                to_x(zz, yy).wait_send()


def gathered(hidden, base_qkv, adapter_id, shrink, expand_q, expand_kv):
    dma = pltpu.SemaphoreType.DMA
    vmem, anywhere = pl.BlockSpec(memory_space=pltpu.VMEM), pl.BlockSpec(memory_space=pl.ANY)
    bf16 = jnp.bfloat16
    return pl.pallas_call(
        exchange,
        out_shape=jax.ShapeDtypeStruct((ROW_DEV, QKV), bf16),
        in_specs=[vmem, anywhere, anywhere, anywhere, anywhere, anywhere],
        out_specs=anywhere,
        scratch_shapes=[
            pltpu.VMEM((PEERS * R, QKV), bf16),
            pltpu.VMEM((SLOTS, D), bf16),
            pltpu.VMEM((SLOTS, D), bf16),
            pltpu.VMEM((3 * R, D), bf16),
            pltpu.VMEM((ROW_DEV, QKV), bf16),
            pltpu.VMEM((8 * CAP, 3 * R), jnp.float32),
            pltpu.VMEM((SLOTS, 6 * R), bf16),
            pltpu.VMEM((SLOTS, 6 * R), bf16),
            pltpu.VMEM((3, ROW_DEV, PEERS * R), bf16),
            pltpu.VMEM((ROW_DEV, QKV), jnp.float32),
            pltpu.VMEM((ROW_DEV, D), bf16),
            pltpu.VMEM((ROW_DEV, QKV), bf16),
            dma((7,)),
            dma((PEERS,)),
            dma((PEERS,)),
            dma((PEERS,)),
            dma((PEERS,)),
            dma((PEERS, 2)),
            dma((Z, 2)),
            dma((Z,)),
            dma((Z, Y)),
            dma((Z, Y, 2)),
            dma((QKV // WIDE,)),
        ],
        compiler_params=pltpu.CompilerParams(
            collective_id=0, has_side_effects=True, vmem_limit_bytes=56 * 1024 * 1024
        ),
        cost_estimate=pl.CostEstimate(flops=4 * 10**9, bytes_accessed=12 * 10**6, transcendentals=0),
    )(
        adapter_id.reshape(1, ROW_DEV), hidden, base_qkv, jnp.swapaxes(shrink, 1, 2), expand_q, expand_kv
    )


def fits(mesh, hidden, shrink, expand_q):
    groups, peers = mesh.shape["group"], mesh.shape["adapter"]
    return (
        (groups, peers) == (2, PEERS)
        and hidden.shape == (groups * peers * ROW_DEV, D)
        and shrink.shape == (PEERS, D, 3 * R)
        and expand_q.shape == (PEERS, R, D)
    )


def solution(mesh):
    placed = (
        P(("group", "adapter"), None),
        P(("group", "adapter"), None),
        P(("group", "adapter"), None),
        P("adapter", None, None),
        P("adapter", None, None),
        P("adapter", None, None, None),
    )

    def whole(hidden, base_qkv, adapter_id, shrink, expand_q, expand_kv):
        body = gathered if fits(mesh, hidden, shrink, expand_q) else per_device
        return mapped(body)(hidden, base_qkv, adapter_id, shrink, expand_q, expand_kv)

    mapped = lambda body: jax.shard_map(
        body,
        mesh=mesh,
        in_specs=placed,
        out_specs=P(("group", "adapter"), None),
        check_vma=False,
    )
    return whole
```
